32 devices in a mesh: grp: 8 (over z, y), head: 4 (over x, core).
Axes of the slice: x: 2, y: 2, z: 4, core: 2. Of those that a mesh axis runs over, the one named last changes fastest.
Arguments:
- activations: bfloat16 [256, 4096], P('grp', 'head'), may hold values from -1.5 to 1.5
- ln_gain: bfloat16 [4096], replicated, may hold values from 0.099609375 to 1.8984375
- ln_bias: bfloat16 [4096], replicated, may hold values from -3 to 3
- w_qkv: bfloat16 [4096, 3, 4096], P('grp', None, 'head'), may hold values from -0.09375 to 0.09375
- prefix_keys: bfloat16 [16, 1024, 4096], P('grp', None, 'head')
- prefix_values: bfloat16 [16, 1024, 4096], P('grp', None, 'head'), may hold values from -6 to 6
- own_keys: bfloat16 [256, 32, 4096], P('grp', None, 'head'), may hold values from -6 to 6
- own_values: bfloat16 [256, 32, 4096], P('grp', None, 'head'), may hold values from -6 to 6
- prompt_len: int32 [16], P('grp'), may hold values from 64 to 1024, as said below
- own_len: int32 [256], P('grp'), may hold values from 1 to 32, as said below
- w_attn_out: bfloat16 [256, 16, 4096], P('grp', 'head'), may hold values from -0.09375 to 0.09375
- w_in: bfloat16 [4096, 16384], P(None, ('grp', 'head')), may hold values from -0.09375 to 0.09375
- b_in: bfloat16 [16384], P(('grp', 'head')), may hold values from -4 to 4
- w_down: bfloat16 [16384, 4096], P(('grp', 'head')), may hold values from -0.046875 to 0.046875
- b_down: bfloat16 [4096], P('head'), may hold values from -3 to 3
Outputs:
- layer_out: bfloat16 [256, 4096], P('grp', 'head')
The draws below stay inside these ranges and needn't reach their ends.
Inputs may be any that keep to these rules, and one draw needn't show every extreme that they name: `prompt_len`: some group's prompt has exactly 1024 tokens and some has 64. `own_len`: some request has exactly 32 own tokens.
All inputs are finite; a program needn't handle non-finite values.
Results may differ from the reference program's by a relative error of at most 0.034.
Values may be sent and summed in bfloat16 or wider, within the bound.
A program may use at most 128 MiB of HBM per device.

```python
import math
import jax
import jax.numpy as jnp
from jax import lax

D = 4096
HEADS = 16
HS = 256
ROT = 64
FF = 16384
GSIZE = 16
OWN = 32
PMAX = 1024
GROUPS = 16
REQS = 256
N_GRP = 8


def draw_prompt_len(key, part):
    first, second, third = jax.random.split(key, 3)
    lowest = PMAX // 16
    spread = jax.random.randint(first, (GROUPS,), 0, 257)
    lengths = lowest + (PMAX - lowest) * spread * spread // 65536
    top = jax.random.randint(second, (), 0, GROUPS)
    bottom = (top + 1 + jax.random.randint(third, (), 0, GROUPS - 1)) % GROUPS
    places = jnp.arange(GROUPS)
    lengths = jnp.where(places == top, PMAX, lengths)
    lengths = jnp.where(places == bottom, lowest, lengths)
    return lengths.astype(jnp.int32)


def draw_own_len(key, part):
    first, second = jax.random.split(key)
    counts = jax.random.randint(first, (REQS,), 1, OWN + 1)
    top = jax.random.randint(second, (), 0, REQS)
    return jnp.where(jnp.arange(REQS) == top, OWN, counts).astype(jnp.int32)


def draw_prefix_keys(key, part):
    first = jax.random.fold_in(key, 0)
    base = jnp.clip(jax.random.normal(first, (GROUPS, PMAX, D), jnp.float32), -4.0, 4.0)
    return base.astype(jnp.bfloat16)


def level_of(key, dims, shards, least, high):
    factor_of = 1.0
    for dim, shards_of in shards:
        heights = jax.random.uniform(jax.random.fold_in(jax.random.fold_in(key, 6), dim), (shards_of,), jnp.float32, least / len(shards), high / len(shards))
        factor_of = factor_of * jnp.repeat(jnp.exp(heights), dims[dim] // shards_of).reshape((-1,) + (1,) * (len(dims) - 1 - dim))
    return factor_of


def bell_draw(stream_key, extent, scale, reach, shards=(), held_as=jnp.bfloat16):
    level = level_of(stream_key, extent, shards, -0.22, 0.18) if shards else 1.0
    result = jax.random.normal(stream_key, extent, jnp.float32) * scale * level
    return jnp.minimum(jnp.maximum(result, -reach), reach).astype(held_as)


def setup_inputs(seed: int = 0) -> dict:
    seeds = jax.random.split(jax.random.key(seed), 16)
    return {
        "activations": bell_draw(seeds[0], (REQS, D), 0.25, 1.5, ((0, 8), (1, 4))),
        "ln_gain": jnp.clip(1.0 + 0.18 * jax.random.normal(seeds[1], (D,), jnp.float32), 0.099609375, 1.8984375).astype(jnp.bfloat16),
        "ln_bias": bell_draw(seeds[2], (D,), 0.5, 3.0),
        "w_qkv": bell_draw(seeds[3], (D, 3, D), D ** -0.5, 0.09375, ((0, 8), (2, 4))),
        "prefix_keys": draw_prefix_keys(jax.random.fold_in(seeds[15], 71), 0),
        "prefix_values": bell_draw(seeds[5], (GROUPS, PMAX, D), 1.0, 6.0, ((0, 8), (2, 4))),
        "own_keys": bell_draw(seeds[6], (REQS, OWN, D), 1.0, 6.0, ((0, 8), (2, 4))),
        "own_values": bell_draw(seeds[7], (REQS, OWN, D), 1.0, 6.0, ((0, 8), (2, 4))),
        "prompt_len": draw_prompt_len(jax.random.fold_in(seeds[15], 71), 0),
        "own_len": draw_own_len(jax.random.fold_in(seeds[15], 71), 0),
        "w_attn_out": bell_draw(seeds[10], (HS, HEADS, D), D ** -0.5, 0.09375, ((0, 8), (1, 4))),
        "w_in": bell_draw(seeds[11], (D, FF), D ** -0.5, 0.09375, ((1, 32),)),
        "b_in": bell_draw(seeds[12], (FF,), 1.0, 4.0, ((0, 32),)),
        "w_down": bell_draw(seeds[13], (FF, D), FF ** -0.5, 0.046875, ((0, 32),)),
        "b_down": bell_draw(seeds[14], (D,), 0.5, 3.0, ((0, 4),)),
    }


def rounded(values):
    return lax.optimization_barrier(values.astype(jnp.bfloat16)).astype(jnp.float32)

def normalize(rows, gain, shift):
    floats = rows.astype(jnp.float32)
    center = floats - lax.optimization_barrier(jnp.mean(floats, axis=-1, keepdims=True))
    spread = lax.optimization_barrier(jnp.mean(center * center, axis=-1, keepdims=True))
    return (center * lax.rsqrt(spread + 1e-05) * gain.astype(jnp.float32) + shift.astype(jnp.float32)).astype(jnp.bfloat16)

def rotate(values, positions):
    half = ROT // 2
    index = jnp.arange(half, dtype=jnp.float32)
    freqs = jnp.power(jnp.float32(10000.0), -2.0 * index / ROT)
    angle = positions[:, None, None] * freqs[None, None, :]
    cosine = jnp.cos(angle)
    sine = jnp.sin(angle)
    pairs = values[..., :ROT].reshape(values.shape[:-1] + (half, 2))
    first = pairs[..., 0]
    second = pairs[..., 1]
    turned = jnp.stack([first * cosine - second * sine, second * cosine + first * sine], axis=-1)
    turned = turned.reshape(values.shape[:-1] + (ROT,))
    return jnp.concatenate([turned, values[..., ROT:]], axis=-1)

def one_group(inputs):
    query, key_new, value_new, pre_keys, pre_vals, mine_keys, mine_vals, plength, olength = inputs
    scale = 1.0 / math.sqrt(HS)
    qfloat = query.astype(jnp.float32)
    pre_keys = pre_keys.reshape(PMAX, HEADS, HS).astype(jnp.float32)
    pre_vals = pre_vals.reshape(PMAX, HEADS, HS).astype(jnp.float32)
    mine_keys = mine_keys.astype(jnp.float32)
    mine_vals = mine_vals.astype(jnp.float32)
    pre_scores = jnp.einsum('qhd,jhd->qhj', qfloat, pre_keys) * scale
    pre_scores = jnp.where(jnp.arange(PMAX)[None, None, :] < plength, pre_scores, -jnp.inf)
    own_scores = jnp.einsum('qhd,qthd->qht', qfloat, mine_keys) * scale
    own_scores = jnp.where(jnp.arange(OWN)[None, None, :] < olength[:, None, None], own_scores, -jnp.inf)
    self_scores = lax.optimization_barrier(jnp.sum(qfloat * key_new.astype(jnp.float32), axis=-1)) * scale
    peak = jnp.maximum(jnp.maximum(lax.optimization_barrier(jnp.max(pre_scores, axis=-1)), lax.optimization_barrier(jnp.max(own_scores, axis=-1))), self_scores)
    pre_exp = jnp.exp(pre_scores - peak[..., None])
    own_exp = jnp.exp(own_scores - peak[..., None])
    self_exp = jnp.exp(self_scores - peak)
    denom = lax.optimization_barrier(jnp.sum(pre_exp, axis=-1)) + lax.optimization_barrier(jnp.sum(own_exp, axis=-1)) + self_exp
    mixed = jnp.einsum('qhj,jhd->qhd', rounded(pre_exp), pre_vals)
    mixed = mixed + jnp.einsum('qht,qthd->qhd', rounded(own_exp), mine_vals)
    mixed = mixed + rounded(self_exp)[..., None] * value_new.astype(jnp.float32)
    return (mixed / denom[..., None]).astype(jnp.bfloat16)

def reference(activations, ln_gain, ln_bias, w_qkv, prefix_keys, prefix_values, own_keys, own_values, prompt_len, own_len, w_attn_out, w_in, b_in, w_down, b_down):
    normed = normalize(activations, ln_gain, ln_bias)
    width = D // N_GRP

    def add_block(running, block):
        rows = lax.dynamic_slice_in_dim(normed, block * width, width, 1)
        weights = lax.dynamic_slice_in_dim(w_qkv, block * width, width, 0)
        term = jnp.einsum('rf,fch->rch', rows.astype(jnp.float32), weights.astype(jnp.float32))
        return (running + rounded(term), None)
    qkv, unused = lax.scan(add_block, jnp.zeros((REQS, 3, D), jnp.float32), jnp.arange(N_GRP, dtype=jnp.int32))
    member = jnp.arange(REQS, dtype=jnp.int32) // GSIZE
    positions = (prompt_len[member] + own_len).astype(jnp.float32)
    query = rotate(qkv[:, 0].reshape(REQS, HEADS, HS), positions).astype(jnp.bfloat16)
    key_new = rotate(qkv[:, 1].reshape(REQS, HEADS, HS), positions).astype(jnp.bfloat16)
    value_new = qkv[:, 2].reshape(REQS, HEADS, HS).astype(jnp.bfloat16)
    attended = lax.map(one_group, (query.reshape(GROUPS, GSIZE, HEADS, HS), key_new.reshape(GROUPS, GSIZE, HEADS, HS), value_new.reshape(GROUPS, GSIZE, HEADS, HS), prefix_keys, prefix_values, own_keys.reshape(GROUPS, GSIZE, OWN, HEADS, HS), own_values.reshape(GROUPS, GSIZE, OWN, HEADS, HS), prompt_len, own_len.reshape(GROUPS, GSIZE)))
    attended = attended.reshape(REQS, HEADS, HS)
    hidden = jax.nn.gelu(jnp.dot(normed, w_in, preferred_element_type=jnp.float32) + b_in.astype(jnp.float32), approximate=True).astype(jnp.bfloat16)
    attn_sum = jnp.einsum('rkd,dko->ro', attended.astype(jnp.float32), w_attn_out.astype(jnp.float32))
    mlp_sum = jnp.dot(hidden, w_down, preferred_element_type=jnp.float32)
    total = activations.astype(jnp.float32) + b_down.astype(jnp.float32) + attn_sum + mlp_sum
    return total.astype(jnp.bfloat16)
```

```python
import functools
import math

import jax
import jax.numpy as jnp
from jax import lax
from jax.experimental import pallas as pl
from jax.experimental.pallas import tpu as pltpu
from jax.sharding import PartitionSpec as P

HS = 256
ROT = 64
GSIZE = 16
MESH = pl.DeviceIdType.MESH
DMA = pltpu.SemaphoreType.DMA
VMEM_SPEC = pl.BlockSpec(memory_space=pltpu.VMEM)
VMEM_LIMIT = 56 * 1024 * 1024


def remote(src, dst, send_sem, recv_sem, device):
    return pltpu.make_async_remote_copy(
        src_ref=src,
        dst_ref=dst,
        send_sem=send_sem,
        recv_sem=recv_sem,
        device_id=device,
        device_id_type=MESH,
    )


def greet(devices):
    barrier = pltpu.get_barrier_semaphore()
    for device in devices:
        pl.semaphore_signal(barrier, inc=1, device_id=device, device_id_type=MESH)
    pl.semaphore_wait(barrier, len(devices))


def place(zs):
    g = lax.axis_index("grp")
    h = lax.axis_index("head")
    return g, h, g // 2, g % 2, h // 2, h % 2


def gather_kernel(zs, heads, act, gain, shift, out, full, hs, hr, zsend, zr, ys, yr, xs, xr, cs, cr, ds_, dr):
    g, h, z, y, x, c = place(zs)
    rows, width = act.shape
    xh = (1 - x) * 2 + c
    ch = x * 2 + (1 - c)
    yg = z * 2 + (1 - y)
    peers = [(g, lax.rem(h + k, heads)) for k in range(1, heads)]
    zpeers = [(lax.rem(z + k, zs) * 2 + y, h) for k in range(1, zs)]
    greet(peers + zpeers + [(yg, h)])

    def columns(ref, quarter):
        return ref.at[:, pl.ds(pl.multiple_of(quarter * width, 128), width)]

    def piece(group, quarter):
        return out.at[
            pl.ds(pl.multiple_of(group * rows, 32), rows),
            pl.ds(pl.multiple_of(quarter * width, 128), width),
        ]

    started = []

    def start(copy):
        copy.start()
        started.append(copy)

    for k in range(1, heads):
        start(remote(act, columns(full, h), hs.at[k], hr.at[k], peers[k - 1]))
    full[:, pl.ds(pl.multiple_of(h * width, 128), width)] = act[...]
    for k in range(1, heads):
        origin = lax.rem(h + heads - k, heads)
        remote(act, columns(full, origin), hs.at[k], hr.at[k], peers[k - 1]).wait_recv()
    floats = full[...].astype(jnp.float32)
    center = floats - jnp.mean(floats, axis=-1, keepdims=True)
    spread = jnp.mean(center * center, axis=-1, keepdims=True)
    normed = center * lax.rsqrt(spread + 1e-05) * gain[...].astype(jnp.float32) + shift[...].astype(
        jnp.float32
    )
    out[pl.ds(pl.multiple_of(g * rows, 32), rows), :] = normed.astype(jnp.bfloat16)

    for k in range(1, zs):
        start(remote(piece(g, h), piece(g, h), zsend.at[k], zr.at[k], zpeers[k - 1]))
    start(remote(piece(g, h), piece(g, h), ys.at[0], yr.at[0], (yg, h)))

    def spread_out(i, group):
        start(remote(piece(group, h), piece(group, h), xs.at[i], xr.at[i], (g, xh)))
        start(remote(piece(group, h), piece(group, h), cs.at[i], cr.at[i], (g, ch)))

    order = []
    for j in range(zs):
        if j > 0:
            group = lax.rem(z + zs - j, zs) * 2 + y
            remote(piece(group, h), piece(group, h), zsend.at[j], zr.at[j], zpeers[j - 1]).wait_recv()
            start(remote(piece(group, h), piece(group, h), ys.at[j], yr.at[j], (yg, h)))
            spread_out(2 * j, group)
            order.append((2 * j, group))
        group = lax.rem(z + zs - j, zs) * 2 + (1 - y)
        remote(piece(group, h), piece(group, h), ys.at[j], yr.at[j], (yg, h)).wait_recv()
        spread_out(2 * j + 1, group)
        order.append((2 * j + 1, group))
    order.sort(key=lambda entry: entry[0] if entry[0] % 2 else entry[0])
    for i, group in order:
        remote(piece(group, xh), piece(group, xh), xs.at[i], xr.at[i], (g, xh)).wait_recv()
        start(remote(piece(group, xh), piece(group, xh), ds_.at[i], dr.at[i], (g, ch)))
    for i, group in order:
        other = (1 - x) * 2 + (1 - c)
        remote(piece(group, ch), piece(group, ch), cs.at[i], cr.at[i], (g, ch)).wait_recv()
        remote(piece(group, other), piece(group, other), ds_.at[i], dr.at[i], (g, ch)).wait_recv()
    for copy in started:
        copy.wait_send()


def gather_normed(activations, gain, shift):
    groups, heads = lax.axis_size("grp"), lax.axis_size("head")
    zs = groups // 2
    rows, width = activations.shape
    scratch = [pltpu.VMEM((rows, width * heads), jnp.bfloat16)]
    scratch += [DMA((heads,))] * 2 + [DMA((zs,))] * 4 + [DMA((groups,))] * 6
    return pl.pallas_call(
        functools.partial(gather_kernel, zs, heads),
        out_shape=jax.ShapeDtypeStruct((groups * rows, heads * width), jnp.bfloat16),
        in_specs=[VMEM_SPEC] * 3,
        out_specs=VMEM_SPEC,
        scratch_shapes=scratch,
        compiler_params=pltpu.CompilerParams(
            collective_id=0, has_side_effects=True, vmem_limit_bytes=VMEM_LIMIT
        ),
        name="gather_normed",
    )(activations, gain.reshape(1, -1), shift.reshape(1, -1))


def qkv_kernel(zs, part, out, r3, s4, r4, ys, yr, zsend, zr):
    g, h, z, y, x, c = place(zs)
    rows = out.shape[1]
    yg = z * 2 + (1 - y)
    zpeers = [(lax.rem(z + k, zs) * 2 + y, h) for k in range(1, zs)]
    greet(zpeers + [(yg, h)])

    def block(k, side):
        group = lax.rem(z + k, zs) * 2 + side
        return pl.ds(pl.multiple_of(group * rows, 32), rows)

    turns = list(range(1, zs)) + [0]
    ycopies = {}
    for k in turns:
        ycopies[k] = remote(part.at[:, block(k, 1 - y), :], r3.at[k], ys.at[k], yr.at[k], (yg, h))
        ycopies[k].start()
    zcopies = []
    for k in range(1, zs):
        ycopies[k].wait_recv()
        pair = part[:, block(k, y), :].astype(jnp.float32) + r3[k].astype(jnp.float32)
        s4[k] = pair.astype(jnp.bfloat16)
        copy = remote(s4.at[k], r4.at[k], zsend.at[k], zr.at[k], zpeers[k - 1])
        copy.start()
        zcopies.append(copy)
    ycopies[0].wait_recv()
    total = part[:, block(0, y), :].astype(jnp.float32) + r3[0].astype(jnp.float32)
    for k in range(1, zs):
        zcopies[k - 1].wait_recv()
        total = total + r4[k].astype(jnp.float32)
    out[...] = total
    for k in turns:
        ycopies[k].wait_send()
    for copy in zcopies:
        copy.wait_send()


def qkv_scatter(part):
    groups = lax.axis_size("grp")
    zs = groups // 2
    rows, width = part.shape[1] // groups, part.shape[2]
    buffer = pltpu.VMEM((zs, 3, rows, width), jnp.bfloat16)
    return pl.pallas_call(
        functools.partial(qkv_kernel, zs),
        out_shape=jax.ShapeDtypeStruct((3, rows, width), jnp.float32),
        in_specs=[VMEM_SPEC],
        out_specs=VMEM_SPEC,
        scratch_shapes=[buffer] * 3 + [DMA((zs,))] * 4,
        compiler_params=pltpu.CompilerParams(
            collective_id=1, has_side_effects=True, vmem_limit_bytes=VMEM_LIMIT
        ),
        name="qkv_scatter",
    )(part)


def out_kernel(zs, part, act, b_down, out, s1, r1, s2, r2, s3, r3, s4, r4, cs, cr, xs, xr, ys, yr, zsend, zr):
    g, h, z, y, x, c = place(zs)
    rows, width = act.shape
    xh = (1 - x) * 2 + c
    ch = x * 2 + (1 - c)
    yg = z * 2 + (1 - y)
    zpeers = [(lax.rem(z + k, zs) * 2 + y, h) for k in range(1, zs)]
    greet(zpeers + [(yg, h), (g, xh), (g, ch)])

    def term(k, ky, quarter):
        side = 1 - y if ky else y
        group = lax.rem(z + k, zs) * 2 + side
        return part[
            pl.ds(pl.multiple_of(group * rows, 32), rows),
            pl.ds(pl.multiple_of(quarter * width, 128), width),
        ]

    turns = list(range(1, zs)) + [0]
    order = [(k, 1) for k in turns] + [(k, 0) for k in turns]
    sends = []
    ccopy, xcopy, ycopy, zcopy = {}, {}, {}, {}
    for k, ky in order:
        i = 2 * k + ky
        s1[i, 0] = term(k, ky, 1 - c).astype(jnp.bfloat16)
        s1[i, 1] = term(k, ky, 3 - c).astype(jnp.bfloat16)
        ccopy[i] = remote(s1.at[i], r1.at[i], cs.at[i], cr.at[i], (g, ch))
        ccopy[i].start()
    for k, ky in order:
        i = 2 * k + ky
        ccopy[i].wait_recv()
        s2[i] = (term(k, ky, xh) + r1[i, 1 - x].astype(jnp.float32)).astype(jnp.bfloat16)
        xcopy[i] = remote(s2.at[i], r2.at[i], xs.at[i], xr.at[i], (g, xh))
        xcopy[i].start()

    def chip_sum(k, ky):
        i = 2 * k + ky
        xcopy[i].wait_recv()
        return term(k, ky, h) + r1[i, x].astype(jnp.float32) + r2[i].astype(jnp.float32)

    for k in turns:
        s3[k] = chip_sum(k, 1).astype(jnp.bfloat16)
        ycopy[k] = remote(s3.at[k], r3.at[k], ys.at[k], yr.at[k], (yg, h))
        ycopy[k].start()
    for k in range(1, zs):
        total = chip_sum(k, 0)
        ycopy[k].wait_recv()
        s4[k] = (total + r3[k].astype(jnp.float32)).astype(jnp.bfloat16)
        zcopy[k] = remote(s4.at[k], r4.at[k], zsend.at[k], zr.at[k], zpeers[k - 1])
        zcopy[k].start()
    total = chip_sum(0, 0) + act[...].astype(jnp.float32) + b_down[...].astype(jnp.float32)
    ycopy[0].wait_recv()
    total = total + r3[0].astype(jnp.float32)
    for k in range(1, zs):
        zcopy[k].wait_recv()
        total = total + r4[k].astype(jnp.float32)
    out[...] = total.astype(jnp.bfloat16)
    for copies in (ccopy, xcopy, ycopy, zcopy):
        for copy in copies.values():
            copy.wait_send()


def out_scatter(part, activations, b_down):
    groups = lax.axis_size("grp")
    zs = groups // 2
    rows, width = activations.shape

    def buffer(*lead):
        return pltpu.VMEM(lead + (rows, width), jnp.bfloat16)

    return pl.pallas_call(
        functools.partial(out_kernel, zs),
        out_shape=jax.ShapeDtypeStruct((rows, width), jnp.bfloat16),
        in_specs=[VMEM_SPEC] * 3,
        out_specs=VMEM_SPEC,
        scratch_shapes=[buffer(groups, 2)] * 2
        + [buffer(groups)] * 2
        + [buffer(zs)] * 4
        + [DMA((groups,))] * 4
        + [DMA((zs,))] * 4,
        compiler_params=pltpu.CompilerParams(
            collective_id=2, has_side_effects=True, vmem_limit_bytes=VMEM_LIMIT
        ),
        name="out_scatter",
    )(part, activations, b_down.reshape(1, -1))


def rotate(values, positions):
    half = ROT // 2
    index = jnp.arange(half, dtype=jnp.float32)
    freqs = jnp.power(jnp.float32(10000.0), -2.0 * index / ROT)
    angle = positions[:, None, None] * freqs[None, None, :]
    cosine = jnp.cos(angle)
    sine = jnp.sin(angle)
    pairs = values[..., :ROT].reshape(values.shape[:-1] + (half, 2))
    first = pairs[..., 0]
    second = pairs[..., 1]
    turned = jnp.stack([first * cosine - second * sine, second * cosine + first * sine], axis=-1)
    turned = turned.reshape(values.shape[:-1] + (ROT,))
    return jnp.concatenate([turned, values[..., ROT:]], axis=-1)


def local(
    activations,
    ln_gain,
    ln_bias,
    w_qkv,
    prefix_keys,
    prefix_values,
    own_keys,
    own_values,
    prompt_len,
    own_len,
    w_attn_out,
    w_in,
    b_in,
    w_down,
    b_down,
):
    grp_count = lax.axis_size("grp")
    head_count = lax.axis_size("head")
    width_here = activations.shape[1]
    local_rows = activations.shape[0]
    groups_here = prompt_len.shape[0]
    gathered = gather_normed(activations, ln_gain, ln_bias)
    features = w_qkv.shape[0]
    columns = lax.dynamic_slice_in_dim(
        gathered, lax.axis_index("grp") * features, features, axis=1
    )
    qkv = qkv_scatter(
        jnp.einsum("rf,fch->crh", columns, w_qkv, preferred_element_type=jnp.float32).astype(
            jnp.bfloat16
        )
    )
    heads_here = w_qkv.shape[2] // HS
    member = (jnp.arange(local_rows) // GSIZE)[:, None] == jnp.arange(groups_here)[None, :]
    row_prompt = jnp.sum(jnp.where(member, prompt_len[None, :], 0), axis=1)
    positions = (row_prompt + own_len).astype(jnp.float32)
    query = rotate(qkv[0].reshape(local_rows, heads_here, HS), positions).astype(jnp.bfloat16)
    key_new = rotate(qkv[1].reshape(local_rows, heads_here, HS), positions).astype(jnp.bfloat16)
    value_new = qkv[2].reshape(local_rows, heads_here, HS).astype(jnp.bfloat16)
    scale = 1.0 / math.sqrt(HS)
    longest = prefix_keys.shape[1]
    own_count = own_keys.shape[1]
    grouped = query.reshape(groups_here, GSIZE, heads_here, HS)
    pre_keys = prefix_keys.reshape(groups_here, longest, heads_here, HS)
    pre_vals = prefix_values.reshape(groups_here, longest, heads_here, HS)
    mine_keys = own_keys.reshape(local_rows, own_count, heads_here, HS)
    mine_vals = own_values.reshape(local_rows, own_count, heads_here, HS)
    pre_scores = (
        jnp.einsum("gqhd,gjhd->gqhj", grouped, pre_keys, preferred_element_type=jnp.float32) * scale
    )
    pre_scores = jnp.where(
        jnp.arange(longest)[None, None, None, :] < prompt_len[:, None, None, None],
        pre_scores,
        -jnp.inf,
    )
    own_scores = (
        jnp.einsum("rhd,rthd->rht", query, mine_keys, preferred_element_type=jnp.float32) * scale
    )
    own_scores = jnp.where(
        jnp.arange(own_count)[None, None, :] < own_len[:, None, None], own_scores, -jnp.inf
    )
    self_scores = (
        jnp.einsum("rhd,rhd->rh", query, key_new, preferred_element_type=jnp.float32) * scale
    )
    pre_peak = jnp.max(pre_scores, axis=-1).reshape(local_rows, heads_here)
    peak = jnp.maximum(jnp.maximum(pre_peak, jnp.max(own_scores, axis=-1)), self_scores)
    pre_exp = jnp.exp(pre_scores - peak.reshape(groups_here, GSIZE, heads_here)[..., None])
    own_exp = jnp.exp(own_scores - peak[..., None])
    self_exp = jnp.exp(self_scores - peak)
    denom = (
        jnp.sum(pre_exp, axis=-1).reshape(local_rows, heads_here)
        + jnp.sum(own_exp, axis=-1)
        + self_exp
    )
    mixed = jnp.einsum(
        "gqhj,gjhd->gqhd",
        pre_exp.astype(jnp.bfloat16),
        pre_vals,
        preferred_element_type=jnp.float32,
    )
    mixed = mixed.reshape(local_rows, heads_here, HS)
    mixed = mixed + jnp.einsum(
        "rht,rthd->rhd", own_exp.astype(jnp.bfloat16), mine_vals, preferred_element_type=jnp.float32
    )
    mixed = mixed + self_exp.astype(jnp.bfloat16).astype(jnp.float32)[..., None] * value_new.astype(
        jnp.float32
    )
    attended = (mixed / denom[..., None]).astype(jnp.bfloat16)
    transposed = jnp.transpose(attended, (2, 1, 0))
    slices = lax.all_to_all(transposed, "grp", split_axis=0, concat_axis=2, tiled=True)
    dim_here = slices.shape[0]
    hidden = jax.nn.gelu(
        jnp.dot(
            gathered,
            w_in,
            preferred_element_type=jnp.float32,
        )
        + b_in.astype(jnp.float32),
        approximate=True,
    ).astype(jnp.bfloat16)
    attn_rows = jnp.transpose(
        slices.reshape(dim_here * heads_here, grp_count * local_rows), (1, 0)
    )
    combined = jnp.dot(hidden, w_down, preferred_element_type=jnp.float32) + jnp.dot(
        attn_rows,
        w_attn_out.reshape(dim_here * heads_here, head_count * width_here),
        preferred_element_type=jnp.float32,
    )
    return out_scatter(combined, activations, b_down)


def solution(mesh):
    in_specs = (
        P("grp", "head"),
        P(),
        P(),
        P("grp", None, "head"),
        P("grp", None, "head"),
        P("grp", None, "head"),
        P("grp", None, "head"),
        P("grp", None, "head"),
        P("grp"),
        P("grp"),
        P("grp", "head", None),
        P(None, ("grp", "head")),
        P(("grp", "head")),
        P(("grp", "head"), None),
        P("head"),
    )
    out_specs = P("grp", "head")
    return jax.shard_map(local, mesh=mesh, in_specs=in_specs, out_specs=out_specs, check_vma=False)
```

```python
import functools
import math

import jax
import jax.numpy as jnp
from jax import lax
from jax.experimental import pallas as pl
from jax.experimental.pallas import tpu as pltpu
from jax.sharding import PartitionSpec as P

HS = 256
ROT = 64
GSIZE = 16
MESH = pl.DeviceIdType.MESH
DMA = pltpu.SemaphoreType.DMA
VMEM_SPEC = pl.BlockSpec(memory_space=pltpu.VMEM)
VMEM_LIMIT = 56 * 1024 * 1024


def remote(src, dst, send_sem, recv_sem, device):
    return pltpu.make_async_remote_copy(
        src_ref=src,
        dst_ref=dst,
        send_sem=send_sem,
        recv_sem=recv_sem,
        device_id=device,
        device_id_type=MESH,
    )


def greet(devices):
    barrier = pltpu.get_barrier_semaphore()
    for device in devices:
        pl.semaphore_signal(barrier, inc=1, device_id=device, device_id_type=MESH)
    pl.semaphore_wait(barrier, len(devices))


def place(zs):
    g = lax.axis_index("grp")
    h = lax.axis_index("head")
    return g, h, g // 2, g % 2, h // 2, h % 2


def gather_kernel(zs, heads, act, affine, out, full, hs, hr, zsend, zr, ys, yr, xs, xr, cs, cr, ds_, dr):
    g, h, z, y, x, c = place(zs)
    rows, width = act.shape
    xh = (1 - x) * 2 + c
    ch = x * 2 + (1 - c)
    yg = z * 2 + (1 - y)
    peers = [(g, lax.rem(h + k, heads)) for k in range(1, heads)]
    zpeers = [(lax.rem(z + k, zs) * 2 + y, h) for k in range(1, zs)]
    greet(peers + zpeers + [(yg, h)])

    def columns(ref, quarter):
        return ref.at[:, pl.ds(pl.multiple_of(quarter * width, 128), width)]

    def piece(group, quarter):
        return out.at[
            pl.ds(pl.multiple_of(group * rows, 32), rows),
            pl.ds(pl.multiple_of(quarter * width, 128), width),
        ]

    started = []

    def start(copy):
        copy.start()
        started.append(copy)

    for k in range(1, heads):
        start(remote(act, columns(full, h), hs.at[k], hr.at[k], peers[k - 1]))
    full[:, pl.ds(pl.multiple_of(h * width, 128), width)] = act[...]
    for k in range(1, heads):
        origin = lax.rem(h + heads - k, heads)
        remote(act, columns(full, origin), hs.at[k], hr.at[k], peers[k - 1]).wait_recv()
    floats = full[...].astype(jnp.float32)
    center = floats - jnp.mean(floats, axis=-1, keepdims=True)
    spread = jnp.mean(center * center, axis=-1, keepdims=True)
    normed = center * lax.rsqrt(spread + 1e-05) * affine[0:1, :] + affine[1:2, :]
    out[pl.ds(pl.multiple_of(g * rows, 32), rows), :] = normed.astype(jnp.bfloat16)

    for k in range(1, zs):
        start(remote(piece(g, h), piece(g, h), zsend.at[k], zr.at[k], zpeers[k - 1]))
    start(remote(piece(g, h), piece(g, h), ys.at[0], yr.at[0], (yg, h)))

    def spread_out(i, group):
        start(remote(piece(group, h), piece(group, h), xs.at[i], xr.at[i], (g, xh)))
        start(remote(piece(group, h), piece(group, h), cs.at[i], cr.at[i], (g, ch)))

    order = []
    for j in range(zs):
        if j > 0:
            group = lax.rem(z + zs - j, zs) * 2 + y
            remote(piece(group, h), piece(group, h), zsend.at[j], zr.at[j], zpeers[j - 1]).wait_recv()
            start(remote(piece(group, h), piece(group, h), ys.at[j], yr.at[j], (yg, h)))
            spread_out(2 * j, group)
            order.append((2 * j, group))
        group = lax.rem(z + zs - j, zs) * 2 + (1 - y)
        remote(piece(group, h), piece(group, h), ys.at[j], yr.at[j], (yg, h)).wait_recv()
        spread_out(2 * j + 1, group)
        order.append((2 * j + 1, group))
    order.sort(key=lambda entry: entry[0] if entry[0] % 2 else entry[0])
    for i, group in order:
        remote(piece(group, xh), piece(group, xh), xs.at[i], xr.at[i], (g, xh)).wait_recv()
        start(remote(piece(group, xh), piece(group, xh), ds_.at[i], dr.at[i], (g, ch)))
    for i, group in order:
        other = (1 - x) * 2 + (1 - c)
        remote(piece(group, ch), piece(group, ch), cs.at[i], cr.at[i], (g, ch)).wait_recv()
        remote(piece(group, other), piece(group, other), ds_.at[i], dr.at[i], (g, ch)).wait_recv()
    for copy in started:
        copy.wait_send()


def gather_normed(activations, gain, shift):
    groups, heads = lax.axis_size("grp"), lax.axis_size("head")
    zs = groups // 2
    rows, width = activations.shape
    scratch = [pltpu.VMEM((rows, width * heads), jnp.bfloat16)]
    scratch += [DMA((heads,))] * 2 + [DMA((zs,))] * 4 + [DMA((groups,))] * 6
    return pl.pallas_call(
        functools.partial(gather_kernel, zs, heads),
        out_shape=jax.ShapeDtypeStruct((groups * rows, heads * width), jnp.bfloat16),
        in_specs=[VMEM_SPEC] * 2,
        out_specs=VMEM_SPEC,
        scratch_shapes=scratch,
        compiler_params=pltpu.CompilerParams(
            collective_id=0, has_side_effects=True, vmem_limit_bytes=VMEM_LIMIT
        ),
        name="gather_normed",
    )(activations, jnp.stack([gain, shift]).astype(jnp.float32))


def qkv_kernel(zs, part, out, r3, s4, r4, ys, yr, zsend, zr):
    g, h, z, y, x, c = place(zs)
    rows = out.shape[1]
    yg = z * 2 + (1 - y)
    zpeers = [(lax.rem(z + k, zs) * 2 + y, h) for k in range(1, zs)]
    greet(zpeers + [(yg, h)])

    def block(k, side):
        group = lax.rem(z + k, zs) * 2 + side
        return pl.ds(pl.multiple_of(group * rows, 32), rows)

    turns = list(range(1, zs)) + [0]
    ycopies = {}
    for k in turns:
        ycopies[k] = remote(part.at[:, block(k, 1 - y), :], r3.at[k], ys.at[k], yr.at[k], (yg, h))
        ycopies[k].start()
    zcopies = []
    for k in range(1, zs):
        ycopies[k].wait_recv()
        pair = part[:, block(k, y), :].astype(jnp.float32) + r3[k].astype(jnp.float32)
        s4[k] = pair.astype(jnp.bfloat16)
        copy = remote(s4.at[k], r4.at[k], zsend.at[k], zr.at[k], zpeers[k - 1])
        copy.start()
        zcopies.append(copy)
    ycopies[0].wait_recv()
    total = part[:, block(0, y), :].astype(jnp.float32) + r3[0].astype(jnp.float32)
    for k in range(1, zs):
        zcopies[k - 1].wait_recv()
        total = total + r4[k].astype(jnp.float32)
    out[...] = total
    for k in turns:
        ycopies[k].wait_send()
    for copy in zcopies:
        copy.wait_send()


def qkv_scatter(part):
    groups = lax.axis_size("grp")
    zs = groups // 2
    rows, width = part.shape[1] // groups, part.shape[2]
    buffer = pltpu.VMEM((zs, 3, rows, width), jnp.bfloat16)
    return pl.pallas_call(
        functools.partial(qkv_kernel, zs),
        out_shape=jax.ShapeDtypeStruct((3, rows, width), jnp.float32),
        in_specs=[VMEM_SPEC],
        out_specs=VMEM_SPEC,
        scratch_shapes=[buffer] * 3 + [DMA((zs,))] * 4,
        compiler_params=pltpu.CompilerParams(
            collective_id=1, has_side_effects=True, vmem_limit_bytes=VMEM_LIMIT
        ),
        name="qkv_scatter",
    )(part)


def out_kernel(zs, part, att, w_out, out, acc, ra, asend, arecv, s1, r1, s2, r2, s3, r3, s4, r4, cs, cr, xs, xr, ys, yr, zsend, zr):
    g, h, z, y, x, c = place(zs)
    rows, width = out.shape
    xh = (1 - x) * 2 + c
    ch = x * 2 + (1 - c)
    yg = z * 2 + (1 - y)
    zpeers = [(lax.rem(z + k, zs) * 2 + y, h) for k in range(1, zs)]
    groups = 2 * zs
    gpeers = [lax.rem(g + k, groups) for k in range(1, groups)]
    greet([(p, h) for p in gpeers] + [(g, xh), (g, ch)])

    def rows_of(group):
        return pl.ds(pl.multiple_of(group * rows, 32), rows)

    acopies = []
    for k in range(1, groups):
        peer = gpeers[k - 1]
        copy = remote(att.at[peer], ra.at[rows_of(g), :], asend.at[k], arecv.at[k], (peer, h))
        copy.start()
        acopies.append(copy)
    ra[rows_of(g), :] = att[g]
    for k in range(1, groups):
        origin = lax.rem(g + groups - k, groups)
        remote(
            att.at[origin], ra.at[rows_of(origin), :], asend.at[k], arecv.at[k], (gpeers[k - 1], h)
        ).wait_recv()
    tile = 512

    @pl.loop(0, part.shape[1] // tile)
    def _(t):
        columns = pl.ds(pl.multiple_of(t * tile, tile), tile)
        acc[:, columns] = part[:, columns] + jnp.dot(
            ra[...], w_out[:, columns], preferred_element_type=jnp.float32
        )

    def term(k, ky, quarter):
        side = 1 - y if ky else y
        group = lax.rem(z + k, zs) * 2 + side
        return acc[
            pl.ds(pl.multiple_of(group * rows, 32), rows),
            pl.ds(pl.multiple_of(quarter * width, 128), width),
        ]

    turns = list(range(1, zs)) + [0]
    order = [(k, 1) for k in turns] + [(k, 0) for k in turns]
    sends = []
    ccopy, xcopy, ycopy, zcopy = {}, {}, {}, {}
    for k, ky in order:
        i = 2 * k + ky
        s1[i, 0] = term(k, ky, 1 - c).astype(jnp.bfloat16)
        s1[i, 1] = term(k, ky, 3 - c).astype(jnp.bfloat16)
        ccopy[i] = remote(s1.at[i], r1.at[i], cs.at[i], cr.at[i], (g, ch))
        ccopy[i].start()
    for k, ky in order:
        i = 2 * k + ky
        ccopy[i].wait_recv()
        s2[i] = (term(k, ky, xh) + r1[i, 1 - x].astype(jnp.float32)).astype(jnp.bfloat16)
        xcopy[i] = remote(s2.at[i], r2.at[i], xs.at[i], xr.at[i], (g, xh))
        xcopy[i].start()

    def chip_sum(k, ky):
        i = 2 * k + ky
        xcopy[i].wait_recv()
        return term(k, ky, h) + r1[i, x].astype(jnp.float32) + r2[i].astype(jnp.float32)

    for k in turns:
        s3[k] = chip_sum(k, 1).astype(jnp.bfloat16)
        ycopy[k] = remote(s3.at[k], r3.at[k], ys.at[k], yr.at[k], (yg, h))
        ycopy[k].start()
    for k in range(1, zs):
        total = chip_sum(k, 0)
        ycopy[k].wait_recv()
        s4[k] = (total + r3[k].astype(jnp.float32)).astype(jnp.bfloat16)
        zcopy[k] = remote(s4.at[k], r4.at[k], zsend.at[k], zr.at[k], zpeers[k - 1])
        zcopy[k].start()
    total = chip_sum(0, 0)
    ycopy[0].wait_recv()
    total = total + r3[0].astype(jnp.float32)
    for k in range(1, zs):
        zcopy[k].wait_recv()
        total = total + r4[k].astype(jnp.float32)
    out[...] = total
    for copy in acopies:
        copy.wait_send()
    for copies in (ccopy, xcopy, ycopy, zcopy):
        for copy in copies.values():
            copy.wait_send()


def out_scatter(part, att, w_out, rows, width):
    groups = lax.axis_size("grp")
    zs = groups // 2
    everyone = groups * rows

    def buffer(*lead):
        return pltpu.VMEM(lead + (rows, width), jnp.bfloat16)

    return pl.pallas_call(
        functools.partial(out_kernel, zs),
        out_shape=jax.ShapeDtypeStruct((rows, width), jnp.float32),
        in_specs=[VMEM_SPEC] * 3,
        out_specs=VMEM_SPEC,
        scratch_shapes=[
            pltpu.VMEM(part.shape, jnp.float32),
            pltpu.VMEM((everyone, att.shape[2]), jnp.bfloat16),
            DMA((groups,)),
            DMA((groups,)),
        ]
        + [buffer(groups, 2)] * 2
        + [buffer(groups)] * 2
        + [buffer(zs)] * 4
        + [DMA((groups,))] * 4
        + [DMA((zs,))] * 4,
        compiler_params=pltpu.CompilerParams(
            collective_id=2, has_side_effects=True, vmem_limit_bytes=VMEM_LIMIT
        ),
        name="out_scatter",
    )(part, att, w_out)


def attention_kernel(own_count, lens, qkv, table, pk, pv, ok, ov, out):
    rows = qkv.shape[1]
    prompt = lens[pl.program_id(0)]
    cosine, sine, own_len = table[0], table[1], table[2][:, 0:1]
    even = lax.broadcasted_iota(jnp.int32, (rows, HS), 1) % 2 == 0

    def turn(values):
        swapped = jnp.where(
            even, pltpu.roll(values, HS - 1, axis=1), pltpu.roll(values, 1, axis=1)
        )
        return (values * cosine + swapped * sine).astype(jnp.bfloat16)

    query = turn(qkv[0])
    key_new = turn(qkv[1])
    value_new = qkv[2].astype(jnp.bfloat16).astype(jnp.float32)
    scale = 1.0 / math.sqrt(HS)
    contract = (((1,), (1,)), ((), ()))
    mine_keys = ok[...].reshape(rows * own_count, HS)
    mine_vals = ov[...].reshape(rows * own_count, HS)
    pre = lax.dot_general(query, pk[0], contract, preferred_element_type=jnp.float32) * scale
    own = lax.dot_general(query, mine_keys, contract, preferred_element_type=jnp.float32) * scale
    me = (
        jnp.sum(query.astype(jnp.float32) * key_new.astype(jnp.float32), axis=1, keepdims=True)
        * scale
    )
    pre = jnp.where(lax.broadcasted_iota(jnp.int32, pre.shape, 1) < prompt, pre, -jnp.inf)
    lane = lax.broadcasted_iota(jnp.int32, own.shape, 1)
    row = lax.broadcasted_iota(jnp.int32, own.shape, 0)
    token = lane - row * own_count
    keep = jnp.logical_and(token >= 0, token.astype(jnp.float32) < own_len)
    own = jnp.where(keep, own, -jnp.inf)
    peak = jnp.maximum(
        jnp.maximum(jnp.max(pre, axis=1, keepdims=True), jnp.max(own, axis=1, keepdims=True)), me
    )
    pre = jnp.exp(pre - peak)
    own = jnp.exp(own - peak)
    me = jnp.exp(me - peak)
    denom = jnp.sum(pre, axis=1, keepdims=True) + jnp.sum(own, axis=1, keepdims=True) + me
    mixed = jnp.dot(pre.astype(jnp.bfloat16), pv[0], preferred_element_type=jnp.float32)
    mixed = mixed + jnp.dot(own.astype(jnp.bfloat16), mine_vals, preferred_element_type=jnp.float32)
    mixed = mixed + me.astype(jnp.bfloat16).astype(jnp.float32) * value_new
    out[...] = (mixed / denom).astype(jnp.bfloat16)


def attention(qkv, prompt_len, own_len, pk, pv, ok, ov):
    rows, width = qkv.shape[1], qkv.shape[2]
    groups, longest = pk.shape[0], pk.shape[1]
    own_count = ok.shape[1]
    member = (jnp.arange(rows) // GSIZE)[:, None] == jnp.arange(groups)[None, :]
    row_prompt = jnp.sum(jnp.where(member, prompt_len[None, :], 0), axis=1)
    positions = (row_prompt + own_len).astype(jnp.float32)
    lane = jnp.arange(HS)
    index = (lane // 2).astype(jnp.float32)
    freqs = jnp.where(lane < ROT, jnp.power(jnp.float32(10000.0), -2.0 * index / ROT), 0.0)
    angle = positions[:, None] * freqs[None, :]
    sign = jnp.where(lane % 2 == 0, -1.0, 1.0)
    table = jnp.stack(
        [
            jnp.cos(angle),
            jnp.sin(angle) * sign[None, :],
            jnp.broadcast_to(own_len.astype(jnp.float32)[:, None], angle.shape),
        ]
    )
    return pl.pallas_call(
        functools.partial(attention_kernel, own_count),
        out_shape=jax.ShapeDtypeStruct((rows, width), jnp.bfloat16),
        grid=(groups, width // HS),
        in_specs=[
            pl.BlockSpec(memory_space=pltpu.SMEM),
            pl.BlockSpec((3, GSIZE, HS), lambda i, j: (0, i, j)),
            pl.BlockSpec((3, GSIZE, HS), lambda i, j: (0, i, 0)),
            pl.BlockSpec((1, longest, HS), lambda i, j: (i, 0, j)),
            pl.BlockSpec((1, longest, HS), lambda i, j: (i, 0, j)),
            pl.BlockSpec((GSIZE, own_count, HS), lambda i, j: (i, 0, j)),
            pl.BlockSpec((GSIZE, own_count, HS), lambda i, j: (i, 0, j)),
        ],
        out_specs=pl.BlockSpec((GSIZE, HS), lambda i, j: (i, j)),
        compiler_params=pltpu.CompilerParams(vmem_limit_bytes=VMEM_LIMIT),
        name="attention",
    )(prompt_len, qkv, table, pk, pv, ok, ov)


def local(
    activations,
    ln_gain,
    ln_bias,
    w_qkv,
    prefix_keys,
    prefix_values,
    own_keys,
    own_values,
    prompt_len,
    own_len,
    w_attn_out,
    w_in,
    b_in,
    w_down,
    b_down,
):
    grp_count = lax.axis_size("grp")
    head_count = lax.axis_size("head")
    width_here = activations.shape[1]
    local_rows = activations.shape[0]
    gathered = gather_normed(activations, ln_gain, ln_bias)
    features = w_qkv.shape[0]
    columns = lax.dynamic_slice_in_dim(
        gathered, lax.axis_index("grp") * features, features, axis=1
    )
    qkv = qkv_scatter(
        jnp.einsum("rf,fch->crh", columns, w_qkv, preferred_element_type=jnp.float32).astype(
            jnp.bfloat16
        )
    )
    heads_here = w_qkv.shape[2] // HS
    attended = attention(
        qkv, prompt_len, own_len, prefix_keys, prefix_values, own_keys, own_values
    )
    dim_here = w_attn_out.shape[0]
    att = jnp.transpose(
        attended.reshape(local_rows, heads_here, grp_count, dim_here), (2, 0, 3, 1)
    ).reshape(grp_count, local_rows, dim_here * heads_here)
    hidden = jax.nn.gelu(
        jnp.dot(
            gathered,
            w_in,
            preferred_element_type=jnp.float32,
        )
        + b_in.astype(jnp.float32),
        approximate=True,
    ).astype(jnp.bfloat16)
    mlp = jnp.dot(hidden, w_down, preferred_element_type=jnp.float32)
    summed = out_scatter(
        mlp,
        att,
        w_attn_out.reshape(dim_here * heads_here, head_count * width_here),
        local_rows,
        width_here,
    )
    total = activations.astype(jnp.float32) + b_down.astype(jnp.float32)[None, :] + summed
    return total.astype(jnp.bfloat16)


def solution(mesh):
    in_specs = (
        P("grp", "head"),
        P(),
        P(),
        P("grp", None, "head"),
        P("grp", None, "head"),
        P("grp", None, "head"),
        P("grp", None, "head"),
        P("grp", None, "head"),
        P("grp"),
        P("grp"),
        P("grp", "head", None),
        P(None, ("grp", "head")),
        P(("grp", "head")),
        P(("grp", "head"), None),
        P("head"),
    )
    out_specs = P("grp", "head")
    return jax.shard_map(local, mesh=mesh, in_specs=in_specs, out_specs=out_specs, check_vma=False)
```

```python
import functools
import math

import jax
import jax.numpy as jnp
from jax import lax
from jax.experimental import pallas as pl
from jax.experimental.pallas import tpu as pltpu
from jax.sharding import PartitionSpec as P

HS = 256
ROT = 64
GSIZE = 16
MESH = pl.DeviceIdType.MESH
DMA = pltpu.SemaphoreType.DMA
VMEM_SPEC = pl.BlockSpec(memory_space=pltpu.VMEM)
VMEM_LIMIT = 56 * 1024 * 1024


def remote(src, dst, send_sem, recv_sem, device):
    return pltpu.make_async_remote_copy(
        src_ref=src,
        dst_ref=dst,
        send_sem=send_sem,
        recv_sem=recv_sem,
        device_id=device,
        device_id_type=MESH,
    )


def greet(devices):
    barrier = pltpu.get_barrier_semaphore()
    for device in devices:
        pl.semaphore_signal(barrier, inc=1, device_id=device, device_id_type=MESH)
    pl.semaphore_wait(barrier, len(devices))


def place(zs):
    g = lax.axis_index("grp")
    h = lax.axis_index("head")
    return g, h, g // 2, g % 2, h // 2, h % 2


def gather_kernel(zs, heads, act, affine, out, full, hs, hr, zsend, zr, ys, yr, xs, xr, cs, cr, ds_, dr):
    g, h, z, y, x, c = place(zs)
    rows, width = act.shape
    xh = (1 - x) * 2 + c
    ch = x * 2 + (1 - c)
    yg = z * 2 + (1 - y)
    peers = [(g, lax.rem(h + k, heads)) for k in range(1, heads)]
    zpeers = [(lax.rem(z + k, zs) * 2 + y, h) for k in range(1, zs)]
    greet(peers + zpeers + [(yg, h)])

    def columns(ref, quarter):
        return ref.at[:, pl.ds(pl.multiple_of(quarter * width, 128), width)]

    def piece(group, quarter):
        return out.at[
            pl.ds(pl.multiple_of(group * rows, 32), rows),
            pl.ds(pl.multiple_of(quarter * width, 128), width),
        ]

    started = []

    def start(copy):
        copy.start()
        started.append(copy)

    for k in range(1, heads):
        start(remote(act, columns(full, h), hs.at[k], hr.at[k], peers[k - 1]))
    full[:, pl.ds(pl.multiple_of(h * width, 128), width)] = act[...]
    for k in range(1, heads):
        origin = lax.rem(h + heads - k, heads)
        remote(act, columns(full, origin), hs.at[k], hr.at[k], peers[k - 1]).wait_recv()
    floats = full[...].astype(jnp.float32)
    center = floats - jnp.mean(floats, axis=-1, keepdims=True)
    spread = jnp.mean(center * center, axis=-1, keepdims=True)
    normed = center * lax.rsqrt(spread + 1e-05) * affine[0:1, :] + affine[1:2, :]
    out[pl.ds(pl.multiple_of(g * rows, 32), rows), :] = normed.astype(jnp.bfloat16)

    for k in range(1, zs):
        start(remote(piece(g, h), piece(g, h), zsend.at[k], zr.at[k], zpeers[k - 1]))
    start(remote(piece(g, h), piece(g, h), ys.at[0], yr.at[0], (yg, h)))

    def spread_out(i, group):
        start(remote(piece(group, h), piece(group, h), xs.at[i], xr.at[i], (g, xh)))
        start(remote(piece(group, h), piece(group, h), cs.at[i], cr.at[i], (g, ch)))

    order = []
    for j in range(zs):
        if j > 0:
            group = lax.rem(z + zs - j, zs) * 2 + y
            remote(piece(group, h), piece(group, h), zsend.at[j], zr.at[j], zpeers[j - 1]).wait_recv()
            start(remote(piece(group, h), piece(group, h), ys.at[j], yr.at[j], (yg, h)))
            spread_out(2 * j, group)
            order.append((2 * j, group))
        group = lax.rem(z + zs - j, zs) * 2 + (1 - y)
        remote(piece(group, h), piece(group, h), ys.at[j], yr.at[j], (yg, h)).wait_recv()
        spread_out(2 * j + 1, group)
        order.append((2 * j + 1, group))
    order.sort(key=lambda entry: entry[0] if entry[0] % 2 else entry[0])
    for i, group in order:
        remote(piece(group, xh), piece(group, xh), xs.at[i], xr.at[i], (g, xh)).wait_recv()
        start(remote(piece(group, xh), piece(group, xh), ds_.at[i], dr.at[i], (g, ch)))
    for i, group in order:
        other = (1 - x) * 2 + (1 - c)
        remote(piece(group, ch), piece(group, ch), cs.at[i], cr.at[i], (g, ch)).wait_recv()
        remote(piece(group, other), piece(group, other), ds_.at[i], dr.at[i], (g, ch)).wait_recv()
    for copy in started:
        copy.wait_send()


def gather_normed(activations, gain, shift):
    groups, heads = lax.axis_size("grp"), lax.axis_size("head")
    zs = groups // 2
    rows, width = activations.shape
    scratch = [pltpu.VMEM((rows, width * heads), jnp.bfloat16)]
    scratch += [DMA((heads,))] * 2 + [DMA((zs,))] * 4 + [DMA((groups,))] * 6
    return pl.pallas_call(
        functools.partial(gather_kernel, zs, heads),
        out_shape=jax.ShapeDtypeStruct((groups * rows, heads * width), jnp.bfloat16),
        in_specs=[VMEM_SPEC] * 2,
        out_specs=VMEM_SPEC,
        scratch_shapes=scratch,
        compiler_params=pltpu.CompilerParams(
            collective_id=0, has_side_effects=True, vmem_limit_bytes=VMEM_LIMIT
        ),
        name="gather_normed",
    )(activations, jnp.stack([gain, shift]).astype(jnp.float32))


def qkv_kernel(
    zs, part, normed, w_in, b_in, w_down, out, mlp, wi, wd, hid, held, r3, s4, r4, ys, yr, zsend, zr
):
    load_in = pltpu.make_async_copy(w_in, wi, held.at[0])
    load_in.start()
    load_down = pltpu.make_async_copy(w_down, wd, held.at[1])
    load_down.start()
    g, h, z, y, x, c = place(zs)
    rows = out.shape[1]
    yg = z * 2 + (1 - y)
    zpeers = [(lax.rem(z + k, zs) * 2 + y, h) for k in range(1, zs)]
    greet(zpeers + [(yg, h)])

    def block(k, side):
        group = lax.rem(z + k, zs) * 2 + side
        return pl.ds(pl.multiple_of(group * rows, 32), rows)

    turns = list(range(1, zs)) + [0]
    ycopies = {}
    for k in turns:
        ycopies[k] = remote(part.at[:, block(k, 1 - y), :], r3.at[k], ys.at[k], yr.at[k], (yg, h))
        ycopies[k].start()
    high = 256
    wide = min(256, wi.shape[1])
    across = wi.shape[1] // wide
    load_in.wait()

    @pl.loop(0, (normed.shape[0] // high) * across)
    def _(t):
        band = pl.ds(pl.multiple_of((t // across) * high, high), high)
        columns = pl.ds(pl.multiple_of((t % across) * wide, wide), wide)
        value = jnp.dot(normed[band, :], wi[:, columns], preferred_element_type=jnp.float32)
        value = value + b_in[:, columns]
        inner = math.sqrt(2.0 / math.pi) * (value + 0.044715 * (value * value * value))
        hid[band, columns] = (0.5 * value * (1.0 + jnp.tanh(inner))).astype(jnp.bfloat16)

    tile = 512
    tiles = wd.shape[1] // tile
    steps = (normed.shape[0] // high) * tiles
    load_down.wait()

    def down(first, last):
        @pl.loop(first, last)
        def _(t):
            band = pl.ds(pl.multiple_of((t // tiles) * high, high), high)
            columns = pl.ds(pl.multiple_of((t % tiles) * tile, tile), tile)
            mlp[band, columns] = jnp.dot(
                hid[band, :], wd[:, columns], preferred_element_type=jnp.float32
            ).astype(mlp.dtype)

    zcopies = []
    for k in range(1, zs):
        ycopies[k].wait_recv()
        pair = part[:, block(k, y), :].astype(jnp.float32) + r3[k].astype(jnp.float32)
        s4[k] = pair.astype(jnp.bfloat16)
        copy = remote(s4.at[k], r4.at[k], zsend.at[k], zr.at[k], zpeers[k - 1])
        copy.start()
        zcopies.append(copy)
        down(steps * (k - 1) // (zs - 1), steps * k // (zs - 1))
    ycopies[0].wait_recv()
    total = part[:, block(0, y), :].astype(jnp.float32) + r3[0].astype(jnp.float32)
    for k in range(1, zs):
        zcopies[k - 1].wait_recv()
        total = total + r4[k].astype(jnp.float32)
    out[...] = total
    for k in turns:
        ycopies[k].wait_send()
    for copy in zcopies:
        copy.wait_send()


def qkv_scatter(part, normed, w_in, b_in, w_down):
    groups = lax.axis_size("grp")
    zs = groups // 2
    rows, width = part.shape[1] // groups, part.shape[2]
    buffer = pltpu.VMEM((zs, 3, rows, width), jnp.bfloat16)
    return pl.pallas_call(
        functools.partial(qkv_kernel, zs),
        out_shape=(
            jax.ShapeDtypeStruct((3, rows, width), jnp.float32),
            jax.ShapeDtypeStruct((part.shape[1], w_down.shape[1]), jnp.bfloat16),
        ),
        in_specs=[
            VMEM_SPEC,
            VMEM_SPEC,
            pl.BlockSpec(memory_space=pl.ANY),
            VMEM_SPEC,
            pl.BlockSpec(memory_space=pl.ANY),
        ],
        out_specs=(VMEM_SPEC, VMEM_SPEC),
        scratch_shapes=[
            pltpu.VMEM(w_in.shape, jnp.bfloat16),
            pltpu.VMEM(w_down.shape, jnp.bfloat16),
            pltpu.VMEM((part.shape[1], w_in.shape[1]), jnp.bfloat16),
            DMA((2,)),
        ]
        + [buffer] * 3
        + [DMA((zs,))] * 4,
        compiler_params=pltpu.CompilerParams(
            collective_id=1, has_side_effects=True, vmem_limit_bytes=VMEM_LIMIT
        ),
        name="qkv_scatter",
    )(part, normed, w_in, b_in.astype(jnp.float32).reshape(1, -1), w_down)


def out_kernel(zs, part, att, w_out, out, acc, ra, asend, arecv, s1, r1, s2, r2, s3, r3, s4, r4, cs, cr, xs, xr, ys, yr, zsend, zr):
    g, h, z, y, x, c = place(zs)
    rows, width = out.shape
    xh = (1 - x) * 2 + c
    ch = x * 2 + (1 - c)
    yg = z * 2 + (1 - y)
    zpeers = [(lax.rem(z + k, zs) * 2 + y, h) for k in range(1, zs)]
    groups = 2 * zs
    gpeers = [lax.rem(g + k, groups) for k in range(1, groups)]
    greet([(p, h) for p in gpeers] + [(g, xh), (g, ch)])

    def rows_of(group):
        return pl.ds(pl.multiple_of(group * rows, 32), rows)

    acopies = []
    for k in range(1, groups):
        peer = gpeers[k - 1]
        copy = remote(att.at[peer], ra.at[rows_of(g), :], asend.at[k], arecv.at[k], (peer, h))
        copy.start()
        acopies.append(copy)
    ra[rows_of(g), :] = att[g]
    for k in range(1, groups):
        origin = lax.rem(g + groups - k, groups)
        remote(
            att.at[origin], ra.at[rows_of(origin), :], asend.at[k], arecv.at[k], (gpeers[k - 1], h)
        ).wait_recv()
    tile = 512

    @pl.loop(0, part.shape[1] // tile)
    def _(t):
        columns = pl.ds(pl.multiple_of(t * tile, tile), tile)
        acc[:, columns] = part[:, columns].astype(jnp.float32) + jnp.dot(
            ra[...], w_out[:, columns], preferred_element_type=jnp.float32
        )

    def term(k, ky, quarter):
        side = 1 - y if ky else y
        group = lax.rem(z + k, zs) * 2 + side
        return acc[
            pl.ds(pl.multiple_of(group * rows, 32), rows),
            pl.ds(pl.multiple_of(quarter * width, 128), width),
        ]

    turns = list(range(1, zs)) + [0]
    order = [(k, 1) for k in turns] + [(k, 0) for k in turns]
    sends = []
    ccopy, xcopy, ycopy, zcopy = {}, {}, {}, {}
    for k, ky in order:
        i = 2 * k + ky
        s1[i, 0] = term(k, ky, 1 - c).astype(jnp.bfloat16)
        s1[i, 1] = term(k, ky, 3 - c).astype(jnp.bfloat16)
        ccopy[i] = remote(s1.at[i], r1.at[i], cs.at[i], cr.at[i], (g, ch))
        ccopy[i].start()
    for k, ky in order:
        i = 2 * k + ky
        ccopy[i].wait_recv()
        s2[i] = (term(k, ky, xh) + r1[i, 1 - x].astype(jnp.float32)).astype(jnp.bfloat16)
        xcopy[i] = remote(s2.at[i], r2.at[i], xs.at[i], xr.at[i], (g, xh))
        xcopy[i].start()

    def chip_sum(k, ky):
        i = 2 * k + ky
        xcopy[i].wait_recv()
        return term(k, ky, h) + r1[i, x].astype(jnp.float32) + r2[i].astype(jnp.float32)

    for k in turns:
        s3[k] = chip_sum(k, 1).astype(jnp.bfloat16)
        ycopy[k] = remote(s3.at[k], r3.at[k], ys.at[k], yr.at[k], (yg, h))
        ycopy[k].start()
    for k in range(1, zs):
        total = chip_sum(k, 0)
        ycopy[k].wait_recv()
        s4[k] = (total + r3[k].astype(jnp.float32)).astype(jnp.bfloat16)
        zcopy[k] = remote(s4.at[k], r4.at[k], zsend.at[k], zr.at[k], zpeers[k - 1])
        zcopy[k].start()
    total = chip_sum(0, 0)
    ycopy[0].wait_recv()
    total = total + r3[0].astype(jnp.float32)
    for k in range(1, zs):
        zcopy[k].wait_recv()
        total = total + r4[k].astype(jnp.float32)
    out[...] = total
    for copy in acopies:
        copy.wait_send()
    for copies in (ccopy, xcopy, ycopy, zcopy):
        for copy in copies.values():
            copy.wait_send()


def out_scatter(part, att, w_out, rows, width):
    groups = lax.axis_size("grp")
    zs = groups // 2
    everyone = groups * rows

    def buffer(*lead):
        return pltpu.VMEM(lead + (rows, width), jnp.bfloat16)

    return pl.pallas_call(
        functools.partial(out_kernel, zs),
        out_shape=jax.ShapeDtypeStruct((rows, width), jnp.float32),
        in_specs=[VMEM_SPEC] * 3,
        out_specs=VMEM_SPEC,
        scratch_shapes=[
            pltpu.VMEM(part.shape, jnp.float32),
            pltpu.VMEM((everyone, att.shape[2]), jnp.bfloat16),
            DMA((groups,)),
            DMA((groups,)),
        ]
        + [buffer(groups, 2)] * 2
        + [buffer(groups)] * 2
        + [buffer(zs)] * 4
        + [DMA((groups,))] * 4
        + [DMA((zs,))] * 4,
        compiler_params=pltpu.CompilerParams(
            collective_id=2, has_side_effects=True, vmem_limit_bytes=VMEM_LIMIT
        ),
        name="out_scatter",
    )(part, att, w_out)


def attention_kernel(own_count, lens, qkv, table, pk, pv, ok, ov, out):
    rows = qkv.shape[1]
    prompt = lens[pl.program_id(0)]
    cosine, sine, own_len = table[0], table[1], table[2][:, 0:1]
    even = lax.broadcasted_iota(jnp.int32, (rows, HS), 1) % 2 == 0

    def turn(values):
        swapped = jnp.where(
            even, pltpu.roll(values, HS - 1, axis=1), pltpu.roll(values, 1, axis=1)
        )
        return (values * cosine + swapped * sine).astype(jnp.bfloat16)

    query = turn(qkv[0])
    key_new = turn(qkv[1])
    value_new = qkv[2].astype(jnp.bfloat16).astype(jnp.float32)
    scale = 1.0 / math.sqrt(HS)
    contract = (((1,), (1,)), ((), ()))
    mine_keys = ok[...].reshape(rows * own_count, HS)
    mine_vals = ov[...].reshape(rows * own_count, HS)
    pre = lax.dot_general(query, pk[0], contract, preferred_element_type=jnp.float32) * scale
    own = lax.dot_general(query, mine_keys, contract, preferred_element_type=jnp.float32) * scale
    me = (
        jnp.sum(query.astype(jnp.float32) * key_new.astype(jnp.float32), axis=1, keepdims=True)
        * scale
    )
    pre = jnp.where(lax.broadcasted_iota(jnp.int32, pre.shape, 1) < prompt, pre, -jnp.inf)
    lane = lax.broadcasted_iota(jnp.int32, own.shape, 1)
    row = lax.broadcasted_iota(jnp.int32, own.shape, 0)
    token = lane - row * own_count
    keep = jnp.logical_and(token >= 0, token.astype(jnp.float32) < own_len)
    own = jnp.where(keep, own, -jnp.inf)
    peak = jnp.maximum(
        jnp.maximum(jnp.max(pre, axis=1, keepdims=True), jnp.max(own, axis=1, keepdims=True)), me
    )
    pre = jnp.exp(pre - peak)
    own = jnp.exp(own - peak)
    me = jnp.exp(me - peak)
    denom = jnp.sum(pre, axis=1, keepdims=True) + jnp.sum(own, axis=1, keepdims=True) + me
    mixed = jnp.dot(pre.astype(jnp.bfloat16), pv[0], preferred_element_type=jnp.float32)
    mixed = mixed + jnp.dot(own.astype(jnp.bfloat16), mine_vals, preferred_element_type=jnp.float32)
    mixed = mixed + me.astype(jnp.bfloat16).astype(jnp.float32) * value_new
    out[...] = (mixed / denom).astype(jnp.bfloat16)


def attention(qkv, prompt_len, own_len, pk, pv, ok, ov):
    rows, width = qkv.shape[1], qkv.shape[2]
    groups, longest = pk.shape[0], pk.shape[1]
    own_count = ok.shape[1]
    member = (jnp.arange(rows) // GSIZE)[:, None] == jnp.arange(groups)[None, :]
    row_prompt = jnp.sum(jnp.where(member, prompt_len[None, :], 0), axis=1)
    positions = (row_prompt + own_len).astype(jnp.float32)
    lane = jnp.arange(HS)
    index = (lane // 2).astype(jnp.float32)
    freqs = jnp.where(lane < ROT, jnp.power(jnp.float32(10000.0), -2.0 * index / ROT), 0.0)
    angle = positions[:, None] * freqs[None, :]
    sign = jnp.where(lane % 2 == 0, -1.0, 1.0)
    table = jnp.stack(
        [
            jnp.cos(angle),
            jnp.sin(angle) * sign[None, :],
            jnp.broadcast_to(own_len.astype(jnp.float32)[:, None], angle.shape),
        ]
    )
    return pl.pallas_call(
        functools.partial(attention_kernel, own_count),
        out_shape=jax.ShapeDtypeStruct((rows, width), jnp.bfloat16),
        grid=(groups, width // HS),
        in_specs=[
            pl.BlockSpec(memory_space=pltpu.SMEM),
            pl.BlockSpec((3, GSIZE, HS), lambda i, j: (0, i, j)),
            pl.BlockSpec((3, GSIZE, HS), lambda i, j: (0, i, 0)),
            pl.BlockSpec((1, longest, HS), lambda i, j: (i, 0, j)),
            pl.BlockSpec((1, longest, HS), lambda i, j: (i, 0, j)),
            pl.BlockSpec((GSIZE, own_count, HS), lambda i, j: (i, 0, j)),
            pl.BlockSpec((GSIZE, own_count, HS), lambda i, j: (i, 0, j)),
        ],
        out_specs=pl.BlockSpec((GSIZE, HS), lambda i, j: (i, j)),
        compiler_params=pltpu.CompilerParams(vmem_limit_bytes=VMEM_LIMIT),
        name="attention",
    )(prompt_len, qkv, table, pk, pv, ok, ov)


def local(
    activations,
    ln_gain,
    ln_bias,
    w_qkv,
    prefix_keys,
    prefix_values,
    own_keys,
    own_values,
    prompt_len,
    own_len,
    w_attn_out,
    w_in,
    b_in,
    w_down,
    b_down,
):
    grp_count = lax.axis_size("grp")
    head_count = lax.axis_size("head")
    width_here = activations.shape[1]
    local_rows = activations.shape[0]
    gathered = gather_normed(activations, ln_gain, ln_bias)
    features = w_qkv.shape[0]
    columns = lax.dynamic_slice_in_dim(
        gathered, lax.axis_index("grp") * features, features, axis=1
    )
    qkv, mlp = qkv_scatter(
        jnp.einsum("rf,fch->crh", columns, w_qkv, preferred_element_type=jnp.float32).astype(
            jnp.bfloat16
        ),
        gathered,
        w_in,
        b_in,
        w_down,
    )
    heads_here = w_qkv.shape[2] // HS
    attended = attention(
        qkv, prompt_len, own_len, prefix_keys, prefix_values, own_keys, own_values
    )
    dim_here = w_attn_out.shape[0]
    att = jnp.transpose(
        attended.reshape(local_rows, heads_here, grp_count, dim_here), (2, 0, 3, 1)
    ).reshape(grp_count, local_rows, dim_here * heads_here)
    summed = out_scatter(
        mlp,
        att,
        w_attn_out.reshape(dim_here * heads_here, head_count * width_here),
        local_rows,
        width_here,
    )
    total = activations.astype(jnp.float32) + b_down.astype(jnp.float32)[None, :] + summed
    return total.astype(jnp.bfloat16)


def solution(mesh):
    in_specs = (
        P("grp", "head"),
        P(),
        P(),
        P("grp", None, "head"),
        P("grp", None, "head"),
        P("grp", None, "head"),
        P("grp", None, "head"),
        P("grp", None, "head"),
        P("grp"),
        P("grp"),
        P("grp", "head", None),
        P(None, ("grp", "head")),
        P(("grp", "head")),
        P(("grp", "head"), None),
        P("head"),
    )
    out_specs = P("grp", "head")
    return jax.shard_map(local, mesh=mesh, in_specs=in_specs, out_specs=out_specs, check_vma=False)
```

```python
import functools
import math

import jax
import jax.numpy as jnp
from jax import lax
from jax.experimental import pallas as pl
from jax.experimental.pallas import tpu as pltpu
from jax.sharding import PartitionSpec as P

HS = 256
ROT = 64
GSIZE = 16
MESH = pl.DeviceIdType.MESH
DMA = pltpu.SemaphoreType.DMA
VMEM_SPEC = pl.BlockSpec(memory_space=pltpu.VMEM)
VMEM_LIMIT = 56 * 1024 * 1024


def remote(src, dst, send_sem, recv_sem, device):
    return pltpu.make_async_remote_copy(
        src_ref=src,
        dst_ref=dst,
        send_sem=send_sem,
        recv_sem=recv_sem,
        device_id=device,
        device_id_type=MESH,
    )


def greet(devices):
    barrier = pltpu.get_barrier_semaphore()
    for device in devices:
        pl.semaphore_signal(barrier, inc=1, device_id=device, device_id_type=MESH)
    pl.semaphore_wait(barrier, len(devices))


def place(zs):
    g = lax.axis_index("grp")
    h = lax.axis_index("head")
    return g, h, g // 2, g % 2, h // 2, h % 2


def gather_kernel(zs, heads, act, affine, out, full, hs, hr, zsend, zr, ys, yr, xs, xr, cs, cr, ds_, dr):
    g, h, z, y, x, c = place(zs)
    rows, width = act.shape
    xh = (1 - x) * 2 + c
    ch = x * 2 + (1 - c)
    yg = z * 2 + (1 - y)
    peers = [(g, lax.rem(h + k, heads)) for k in range(1, heads)]
    zpeers = [(lax.rem(z + k, zs) * 2 + y, h) for k in range(1, zs)]
    greet(peers + zpeers + [(yg, h)])

    def columns(ref, quarter):
        return ref.at[:, pl.ds(pl.multiple_of(quarter * width, 128), width)]

    def piece(group, quarter):
        return out.at[
            pl.ds(pl.multiple_of(group * rows, 32), rows),
            pl.ds(pl.multiple_of(quarter * width, 128), width),
        ]

    started = []

    def start(copy):
        copy.start()
        started.append(copy)

    for k in range(1, heads):
        start(remote(act, columns(full, h), hs.at[k], hr.at[k], peers[k - 1]))
    full[:, pl.ds(pl.multiple_of(h * width, 128), width)] = act[...]
    for k in range(1, heads):
        origin = lax.rem(h + heads - k, heads)
        remote(act, columns(full, origin), hs.at[k], hr.at[k], peers[k - 1]).wait_recv()
    floats = full[...].astype(jnp.float32)
    center = floats - jnp.mean(floats, axis=-1, keepdims=True)
    spread = jnp.mean(center * center, axis=-1, keepdims=True)
    normed = center * lax.rsqrt(spread + 1e-05) * affine[0:1, :] + affine[1:2, :]
    out[pl.ds(pl.multiple_of(g * rows, 32), rows), :] = normed.astype(jnp.bfloat16)

    for k in range(1, zs):
        start(remote(piece(g, h), piece(g, h), zsend.at[k], zr.at[k], zpeers[k - 1]))
    start(remote(piece(g, h), piece(g, h), ys.at[0], yr.at[0], (yg, h)))

    def spread_out(i, group):
        start(remote(piece(group, h), piece(group, h), xs.at[i], xr.at[i], (g, xh)))
        start(remote(piece(group, h), piece(group, h), cs.at[i], cr.at[i], (g, ch)))

    order = []
    for j in range(zs):
        if j > 0:
            group = lax.rem(z + zs - j, zs) * 2 + y
            remote(piece(group, h), piece(group, h), zsend.at[j], zr.at[j], zpeers[j - 1]).wait_recv()
            start(remote(piece(group, h), piece(group, h), ys.at[j], yr.at[j], (yg, h)))
            spread_out(2 * j, group)
            order.append((2 * j, group))
        group = lax.rem(z + zs - j, zs) * 2 + (1 - y)
        remote(piece(group, h), piece(group, h), ys.at[j], yr.at[j], (yg, h)).wait_recv()
        spread_out(2 * j + 1, group)
        order.append((2 * j + 1, group))
    order.sort(key=lambda entry: entry[0] if entry[0] % 2 else entry[0])
    for i, group in order:
        remote(piece(group, xh), piece(group, xh), xs.at[i], xr.at[i], (g, xh)).wait_recv()
        start(remote(piece(group, xh), piece(group, xh), ds_.at[i], dr.at[i], (g, ch)))
    for i, group in order:
        other = (1 - x) * 2 + (1 - c)
        remote(piece(group, ch), piece(group, ch), cs.at[i], cr.at[i], (g, ch)).wait_recv()
        remote(piece(group, other), piece(group, other), ds_.at[i], dr.at[i], (g, ch)).wait_recv()
    for copy in started:
        copy.wait_send()


def gather_normed(activations, gain, shift):
    groups, heads = lax.axis_size("grp"), lax.axis_size("head")
    zs = groups // 2
    rows, width = activations.shape
    scratch = [pltpu.VMEM((rows, width * heads), jnp.bfloat16)]
    scratch += [DMA((heads,))] * 2 + [DMA((zs,))] * 4 + [DMA((groups,))] * 6
    return pl.pallas_call(
        functools.partial(gather_kernel, zs, heads),
        out_shape=jax.ShapeDtypeStruct((groups * rows, heads * width), jnp.bfloat16),
        in_specs=[VMEM_SPEC] * 2,
        out_specs=VMEM_SPEC,
        scratch_shapes=scratch,
        compiler_params=pltpu.CompilerParams(
            collective_id=0, has_side_effects=True, vmem_limit_bytes=VMEM_LIMIT
        ),
        name="gather_normed",
    )(activations, jnp.stack([gain.astype(jnp.float32), shift.astype(jnp.float32)]))


def qkv_kernel(
    zs, part, normed, w_in, b_in, w_down, out, mlp, wi, wd, hid, held, r3, s4, r4, ys, yr, zsend, zr
):
    load_in = pltpu.make_async_copy(w_in, wi, held.at[0])
    load_in.start()
    load_down = pltpu.make_async_copy(w_down, wd, held.at[1])
    load_down.start()
    g, h, z, y, x, c = place(zs)
    rows = out.shape[1]
    yg = z * 2 + (1 - y)
    zpeers = [(lax.rem(z + k, zs) * 2 + y, h) for k in range(1, zs)]
    greet(zpeers + [(yg, h)])

    def block(k, side):
        group = lax.rem(z + k, zs) * 2 + side
        return pl.ds(pl.multiple_of(group * rows, 32), rows)

    turns = list(range(1, zs)) + [0]
    ycopies = {}
    for k in turns:
        ycopies[k] = remote(part.at[:, block(k, 1 - y), :], r3.at[k], ys.at[k], yr.at[k], (yg, h))
        ycopies[k].start()
    high = 256
    wide = min(256, wi.shape[1])
    across = wi.shape[1] // wide
    load_in.wait()

    @pl.loop(0, (normed.shape[0] // high) * across)
    def _(t):
        band = pl.ds(pl.multiple_of((t // across) * high, high), high)
        columns = pl.ds(pl.multiple_of((t % across) * wide, wide), wide)
        value = jnp.dot(normed[band, :], wi[:, columns], preferred_element_type=jnp.float32)
        value = value + b_in[:, columns]
        inner = math.sqrt(2.0 / math.pi) * (value + 0.044715 * (value * value * value))
        hid[band, columns] = (0.5 * value * (1.0 + jnp.tanh(inner))).astype(jnp.bfloat16)

    tile = 512
    tiles = wd.shape[1] // tile
    steps = (normed.shape[0] // high) * tiles
    load_down.wait()

    def down(first, last):
        @pl.loop(first, last)
        def _(t):
            band = pl.ds(pl.multiple_of((t // tiles) * high, high), high)
            columns = pl.ds(pl.multiple_of((t % tiles) * tile, tile), tile)
            mlp[band, columns] = jnp.dot(
                hid[band, :], wd[:, columns], preferred_element_type=jnp.float32
            ).astype(mlp.dtype)

    zcopies = []
    for k in range(1, zs):
        ycopies[k].wait_recv()
        pair = part[:, block(k, y), :].astype(jnp.float32) + r3[k].astype(jnp.float32)
        s4[k] = pair.astype(jnp.bfloat16)
        copy = remote(s4.at[k], r4.at[k], zsend.at[k], zr.at[k], zpeers[k - 1])
        copy.start()
        zcopies.append(copy)
        down(steps * (k - 1) // (zs - 1), steps * k // (zs - 1))
    ycopies[0].wait_recv()
    total = part[:, block(0, y), :].astype(jnp.float32) + r3[0].astype(jnp.float32)
    for k in range(1, zs):
        zcopies[k - 1].wait_recv()
        total = total + r4[k].astype(jnp.float32)
    out[...] = total
    for k in turns:
        ycopies[k].wait_send()
    for copy in zcopies:
        copy.wait_send()


def qkv_scatter(part, normed, w_in, b_in, w_down):
    groups = lax.axis_size("grp")
    zs = groups // 2
    rows, width = part.shape[1] // groups, part.shape[2]
    buffer = pltpu.VMEM((zs, 3, rows, width), jnp.bfloat16)
    return pl.pallas_call(
        functools.partial(qkv_kernel, zs),
        out_shape=(
            jax.ShapeDtypeStruct((3, rows, width), jnp.float32),
            jax.ShapeDtypeStruct((part.shape[1], w_down.shape[1]), jnp.bfloat16),
        ),
        in_specs=[
            VMEM_SPEC,
            VMEM_SPEC,
            pl.BlockSpec(memory_space=pl.ANY),
            VMEM_SPEC,
            pl.BlockSpec(memory_space=pl.ANY),
        ],
        out_specs=(VMEM_SPEC, VMEM_SPEC),
        scratch_shapes=[
            pltpu.VMEM(w_in.shape, jnp.bfloat16),
            pltpu.VMEM(w_down.shape, jnp.bfloat16),
            pltpu.VMEM((part.shape[1], w_in.shape[1]), jnp.bfloat16),
            DMA((2,)),
        ]
        + [buffer] * 3
        + [DMA((zs,))] * 4,
        compiler_params=pltpu.CompilerParams(
            collective_id=1, has_side_effects=True, vmem_limit_bytes=VMEM_LIMIT
        ),
        name="qkv_scatter",
    )(part, normed, w_in, b_in.astype(jnp.float32).reshape(1, -1), w_down)


def out_kernel(zs, part, att, w_out, out, acc, ra, asend, arecv, s1, r1, s2, r2, s3, r3, s4, r4, cs, cr, xs, xr, ys, yr, zsend, zr):
    g, h, z, y, x, c = place(zs)
    rows, width = out.shape
    xh = (1 - x) * 2 + c
    ch = x * 2 + (1 - c)
    yg = z * 2 + (1 - y)
    zpeers = [(lax.rem(z + k, zs) * 2 + y, h) for k in range(1, zs)]
    groups = 2 * zs
    gpeers = [lax.rem(g + k, groups) for k in range(1, groups)]
    greet([(p, h) for p in gpeers] + [(g, xh), (g, ch)])

    def rows_of(group):
        return pl.ds(pl.multiple_of(group * rows, 32), rows)

    acopies = []
    for k in range(1, groups):
        peer = gpeers[k - 1]
        copy = remote(att.at[peer], ra.at[rows_of(g), :], asend.at[k], arecv.at[k], (peer, h))
        copy.start()
        acopies.append(copy)
    ra[rows_of(g), :] = att[g]
    for k in range(1, groups):
        origin = lax.rem(g + groups - k, groups)
        remote(
            att.at[origin], ra.at[rows_of(origin), :], asend.at[k], arecv.at[k], (gpeers[k - 1], h)
        ).wait_recv()
    tile = 512

    @pl.loop(0, part.shape[1] // tile)
    def _(t):
        columns = pl.ds(pl.multiple_of(t * tile, tile), tile)
        acc[:, columns] = part[:, columns].astype(jnp.float32) + jnp.dot(
            ra[...], w_out[:, columns], preferred_element_type=jnp.float32
        )

    def term(k, ky, quarter):
        side = 1 - y if ky else y
        group = lax.rem(z + k, zs) * 2 + side
        return acc[
            pl.ds(pl.multiple_of(group * rows, 32), rows),
            pl.ds(pl.multiple_of(quarter * width, 128), width),
        ]

    turns = list(range(1, zs)) + [0]
    order = [(k, 1) for k in turns] + [(k, 0) for k in turns]
    sends = []
    ccopy, xcopy, ycopy, zcopy = {}, {}, {}, {}
    for k, ky in order:
        i = 2 * k + ky
        s1[i, 0] = term(k, ky, 1 - c).astype(jnp.bfloat16)
        s1[i, 1] = term(k, ky, 3 - c).astype(jnp.bfloat16)
        ccopy[i] = remote(s1.at[i], r1.at[i], cs.at[i], cr.at[i], (g, ch))
        ccopy[i].start()
    for k, ky in order:
        i = 2 * k + ky
        ccopy[i].wait_recv()
        s2[i] = (term(k, ky, xh) + r1[i, 1 - x].astype(jnp.float32)).astype(jnp.bfloat16)
        xcopy[i] = remote(s2.at[i], r2.at[i], xs.at[i], xr.at[i], (g, xh))
        xcopy[i].start()

    def chip_sum(k, ky):
        i = 2 * k + ky
        xcopy[i].wait_recv()
        return term(k, ky, h) + r1[i, x].astype(jnp.float32) + r2[i].astype(jnp.float32)

    for k in turns:
        s3[k] = chip_sum(k, 1).astype(jnp.bfloat16)
        ycopy[k] = remote(s3.at[k], r3.at[k], ys.at[k], yr.at[k], (yg, h))
        ycopy[k].start()
    for k in range(1, zs):
        total = chip_sum(k, 0)
        ycopy[k].wait_recv()
        s4[k] = (total + r3[k].astype(jnp.float32)).astype(jnp.bfloat16)
        zcopy[k] = remote(s4.at[k], r4.at[k], zsend.at[k], zr.at[k], zpeers[k - 1])
        zcopy[k].start()
    total = chip_sum(0, 0)
    ycopy[0].wait_recv()
    total = total + r3[0].astype(jnp.float32)
    for k in range(1, zs):
        zcopy[k].wait_recv()
        total = total + r4[k].astype(jnp.float32)
    out[...] = total
    for copy in acopies:
        copy.wait_send()
    for copies in (ccopy, xcopy, ycopy, zcopy):
        for copy in copies.values():
            copy.wait_send()


def out_scatter(part, att, w_out, rows, width):
    groups = lax.axis_size("grp")
    zs = groups // 2
    everyone = groups * rows

    def buffer(*lead):
        return pltpu.VMEM(lead + (rows, width), jnp.bfloat16)

    return pl.pallas_call(
        functools.partial(out_kernel, zs),
        out_shape=jax.ShapeDtypeStruct((rows, width), jnp.float32),
        in_specs=[VMEM_SPEC] * 3,
        out_specs=VMEM_SPEC,
        scratch_shapes=[
            pltpu.VMEM(part.shape, jnp.float32),
            pltpu.VMEM((everyone, att.shape[2]), jnp.bfloat16),
            DMA((groups,)),
            DMA((groups,)),
        ]
        + [buffer(groups, 2)] * 2
        + [buffer(groups)] * 2
        + [buffer(zs)] * 4
        + [DMA((groups,))] * 4
        + [DMA((zs,))] * 4,
        compiler_params=pltpu.CompilerParams(
            collective_id=2, has_side_effects=True, vmem_limit_bytes=VMEM_LIMIT
        ),
        name="out_scatter",
    )(part, att, w_out)


def attention_kernel(own_count, lens, qkv, table, pk, pv, ok, ov, out):
    rows = qkv.shape[1]
    prompt = lens[pl.program_id(0)]
    cosine, sine, own_len = table[0], table[1], table[2][:, 0:1]
    even = lax.broadcasted_iota(jnp.int32, (rows, HS), 1) % 2 == 0

    def turn(values):
        swapped = jnp.where(
            even, pltpu.roll(values, HS - 1, axis=1), pltpu.roll(values, 1, axis=1)
        )
        return (values * cosine + swapped * sine).astype(jnp.bfloat16)

    query = turn(qkv[0])
    key_new = turn(qkv[1])
    value_new = qkv[2].astype(jnp.bfloat16).astype(jnp.float32)
    scale = 1.0 / math.sqrt(HS)
    contract = (((1,), (1,)), ((), ()))
    mine_keys = ok[...].reshape(rows * own_count, HS)
    mine_vals = ov[...].reshape(rows * own_count, HS)
    pre = lax.dot_general(query, pk[0], contract, preferred_element_type=jnp.float32) * scale
    own = lax.dot_general(query, mine_keys, contract, preferred_element_type=jnp.float32) * scale
    me = (
        jnp.sum(query.astype(jnp.float32) * key_new.astype(jnp.float32), axis=1, keepdims=True)
        * scale
    )
    pre = jnp.where(lax.broadcasted_iota(jnp.int32, pre.shape, 1) < prompt, pre, -jnp.inf)
    lane = lax.broadcasted_iota(jnp.int32, own.shape, 1)
    row = lax.broadcasted_iota(jnp.int32, own.shape, 0)
    token = lane - row * own_count
    keep = jnp.logical_and(token >= 0, token.astype(jnp.float32) < own_len)
    own = jnp.where(keep, own, -jnp.inf)
    peak = jnp.maximum(
        jnp.maximum(jnp.max(pre, axis=1, keepdims=True), jnp.max(own, axis=1, keepdims=True)), me
    )
    pre = jnp.exp(pre - peak)
    own = jnp.exp(own - peak)
    me = jnp.exp(me - peak)
    denom = jnp.sum(pre, axis=1, keepdims=True) + jnp.sum(own, axis=1, keepdims=True) + me
    mixed = jnp.dot(pre.astype(jnp.bfloat16), pv[0], preferred_element_type=jnp.float32)
    mixed = mixed + jnp.dot(own.astype(jnp.bfloat16), mine_vals, preferred_element_type=jnp.float32)
    mixed = mixed + me.astype(jnp.bfloat16).astype(jnp.float32) * value_new
    out[...] = (mixed / denom).astype(jnp.bfloat16)


def attention(qkv, prompt_len, own_len, pk, pv, ok, ov):
    rows, width = qkv.shape[1], qkv.shape[2]
    groups, longest = pk.shape[0], pk.shape[1]
    own_count = ok.shape[1]
    member = (jnp.arange(rows) // GSIZE)[:, None] == jnp.arange(groups)[None, :]
    row_prompt = jnp.sum(jnp.where(member, prompt_len[None, :], 0), axis=1)
    positions = (row_prompt + own_len).astype(jnp.float32)
    lane = jnp.arange(HS)
    index = (lane // 2).astype(jnp.float32)
    freqs = jnp.where(lane < ROT, jnp.power(jnp.float32(10000.0), -2.0 * index / ROT), 0.0)
    angle = positions[:, None] * freqs[None, :]
    sign = jnp.where(lane % 2 == 0, -1.0, 1.0)
    table = jnp.stack(
        [
            jnp.cos(angle),
            jnp.sin(angle) * sign[None, :],
            jnp.broadcast_to(own_len.astype(jnp.float32)[:, None], angle.shape),
        ]
    )
    return pl.pallas_call(
        functools.partial(attention_kernel, own_count),
        out_shape=jax.ShapeDtypeStruct((rows, width), jnp.bfloat16),
        grid=(groups, width // HS),
        in_specs=[
            pl.BlockSpec(memory_space=pltpu.SMEM),
            pl.BlockSpec((3, GSIZE, HS), lambda i, j: (0, i, j)),
            pl.BlockSpec((3, GSIZE, HS), lambda i, j: (0, i, 0)),
            pl.BlockSpec((1, longest, HS), lambda i, j: (i, 0, j)),
            pl.BlockSpec((1, longest, HS), lambda i, j: (i, 0, j)),
            pl.BlockSpec((GSIZE, own_count, HS), lambda i, j: (i, 0, j)),
            pl.BlockSpec((GSIZE, own_count, HS), lambda i, j: (i, 0, j)),
        ],
        out_specs=pl.BlockSpec((GSIZE, HS), lambda i, j: (i, j)),
        compiler_params=pltpu.CompilerParams(vmem_limit_bytes=VMEM_LIMIT),
        name="attention",
    )(prompt_len, qkv, table, pk, pv, ok, ov)


def local(
    activations,
    ln_gain,
    ln_bias,
    w_qkv,
    prefix_keys,
    prefix_values,
    own_keys,
    own_values,
    prompt_len,
    own_len,
    w_attn_out,
    w_in,
    b_in,
    w_down,
    b_down,
):
    grp_count = lax.axis_size("grp")
    head_count = lax.axis_size("head")
    width_here = activations.shape[1]
    local_rows = activations.shape[0]
    gathered = gather_normed(activations, ln_gain, ln_bias)
    features = w_qkv.shape[0]
    columns = lax.dynamic_slice_in_dim(
        gathered, lax.axis_index("grp") * features, features, axis=1
    )
    qkv, mlp = qkv_scatter(
        jnp.einsum("rf,fch->crh", columns, w_qkv, preferred_element_type=jnp.float32).astype(
            jnp.bfloat16
        ),
        gathered,
        w_in,
        b_in,
        w_down,
    )
    heads_here = w_qkv.shape[2] // HS
    attended = attention(
        qkv, prompt_len, own_len, prefix_keys, prefix_values, own_keys, own_values
    )
    dim_here = w_attn_out.shape[0]
    att = jnp.transpose(
        attended.reshape(local_rows, heads_here, grp_count, dim_here), (2, 0, 3, 1)
    ).reshape(grp_count, local_rows, dim_here * heads_here)
    summed = out_scatter(
        mlp,
        att,
        w_attn_out.reshape(dim_here * heads_here, head_count * width_here),
        local_rows,
        width_here,
    )
    total = activations.astype(jnp.float32) + b_down.astype(jnp.float32)[None, :] + summed
    return total.astype(jnp.bfloat16)


def solution(mesh):
    in_specs = (
        P("grp", "head"),
        P(),
        P(),
        P("grp", None, "head"),
        P("grp", None, "head"),
        P("grp", None, "head"),
        P("grp", None, "head"),
        P("grp", None, "head"),
        P("grp"),
        P("grp"),
        P("grp", "head", None),
        P(None, ("grp", "head")),
        P(("grp", "head")),
        P(("grp", "head"), None),
        P("head"),
    )
    out_specs = P("grp", "head")
    return jax.shard_map(local, mesh=mesh, in_specs=in_specs, out_specs=out_specs, check_vma=False)
```
